32 devices in a mesh: grp: 2 (over y), seq: 4 (over z), head: 2 (over x), rep: 2 (over core).
Axes of the slice: x: 2, y: 2, z: 4, core: 2. Of those that a mesh axis runs over, the one named last changes fastest.
Arguments:
- tokens: bfloat16 [16, 2048, 4096], P(('grp', 'rep', 'head'), 'seq'), parts along dimension 0, may hold values from -250 to 250
- w_query: bfloat16 [4096, 2048], P(None, 'head'), may hold values from -0.09375 to 0.09375
- w_out: bfloat16 [2048, 4096], P('head'), may hold values from -0.5 to 0.5
- neighbour_kv: bfloat16 [256, 2, 128, 2048], P(('grp', 'seq', 'rep'), None, None, 'head'), parts along dimension 0, may hold values from -150 to 150
- shard_lists: int32 [16, 32, 2], P(('grp', 'seq', 'rep')), parts along dimension 0, may hold values from 0 to 3, as said below
- slot_lists: int32 [16, 32, 2], P(('grp', 'seq', 'rep')), parts along dimension 0, may hold values from 0 to 15
Outputs:
- crossed: bfloat16 [16, 2048, 4096], P(('grp', 'rep', 'head'), 'seq'), parts along dimension 0
The draws below stay inside these ranges and needn't reach their ends.
There are 2 independent parts, one for each index of `grp`. The reference program is written for one: setup_inputs(seed, part) draws one part's arguments, and reference() takes and returns one part's arrays. A program takes and returns all parts, laid end to end along the dimension named above; an argument that names none is the same for every part. Nothing has to cross between parts.
Inputs may be any that keep to these rules, and one draw needn't show every extreme that they name: `shard_lists`: each entry row names 2 different encoder shards; at most 24 of the 64 entries of one owner name the same shard.
All inputs are finite; a program needn't handle non-finite values.
Results may differ from the reference program's by a relative error of at most 0.0038.
The reference program's roundings to bfloat16 on the way (of `normed`, `queries`, `weights` and `context`) count: a program that leaves them out, or rounds other values in their place, can miss the bound.
Values may be sent and summed in bfloat16 or wider, within the bound.
A program may use at most 256 MiB of HBM per device.

```python
import math
import jax
import jax.numpy as jnp
from jax import lax

D = 4096
HEADS = 16
DH = 128
BLOCK = 64
NLEN = 128
KN = 2
L = 2048
SEQ_REP = 4
HD = 2048
SEQS = 8
SHARD_BLOCKS = 8
OWN_BLOCKS = 32
OWNERS = 8
CAPACITY = 24
STORE_DEV = 16
STORE = 128
N_SEQ = 4
N_HEAD = 2
N_REP = 2


def draw_tokens(key, part):
    key = jax.random.fold_in(key, 11)
    base_key, row_key, column_key = jax.random.split(key, 3)
    sample = jnp.clip(jax.random.normal(base_key, (SEQS, L, D), jnp.float32), -6.0, 6.0)
    row_top = math.log(10.0)
    row_scale = jnp.exp(jax.random.uniform(row_key, (SEQS, L, 1), jnp.float32, 0.0, row_top))
    column_scale = jnp.exp(jax.random.uniform(column_key, (1, 1, D), jnp.float32, -1.15, 1.15))
    return jnp.clip(sample * row_scale * column_scale, -250.0, 250.0).astype(jnp.bfloat16)


def draw_neighbour_kv(key, part):
    key = jax.random.fold_in(key, 23)
    base_key = jax.random.fold_in(key, 0)
    full_shape = (STORE, 2, NLEN, HD)
    sample = jnp.clip(jax.random.normal(base_key, full_shape, jnp.float32), -6.0, 6.0)
    return jnp.clip(sample, -150.0, 150.0).astype(jnp.bfloat16)


def draw_shard_lists(key, part):
    key = jax.random.fold_in(key, 37)
    hot_key, rest_key = jax.random.split(key)
    hot_shard = jax.random.randint(hot_key, (), 0, N_SEQ)

    def one_block(block_key):
        order_key, row_key = jax.random.split(block_key)
        shuffled = jax.random.permutation(order_key, N_SEQ - 1)
        others = jnp.where(shuffled >= hot_shard, shuffled + 1, shuffled)
        pick_index = jnp.arange(OWN_BLOCKS * KN)
        spread_picks = others[jnp.maximum(pick_index - CAPACITY, 0) % (N_SEQ - 1)]
        chosen = jnp.where(pick_index < CAPACITY, hot_shard, spread_picks)
        row_table = chosen.reshape(KN, OWN_BLOCKS).T
        row_order = jax.random.permutation(row_key, OWN_BLOCKS)
        return row_table[row_order]
    block_keys = jax.random.split(rest_key, OWNERS)
    return jax.vmap(one_block)(block_keys).astype(jnp.int32)


def set_ends(entries, key, smallest, largest):
    longest = entries.shape.index(max(entries.shape))
    spots = []
    for shift in (0, 1):
        where = [jax.random.randint(jax.random.fold_in(key, axis), (), 0, length) for axis, length in enumerate(entries.shape)]
        where[longest] = (where[longest] + shift) % entries.shape[longest]
        spots.append(tuple(where))
    return entries.at[spots[0]].set(smallest).at[spots[1]].set(largest)


def block_scale(rng, extent, cuts, least, high):
    def one(dim, parts):
        heights = jax.random.uniform(jax.random.fold_in(jax.random.fold_in(rng, 6), dim), (parts,), jnp.float32, least / len(cuts), high / len(cuts))
        return jnp.repeat(jnp.exp(heights), extent[dim] // parts).reshape((-1,) + (1,) * (len(extent) - dim - 1))

    level = one(*cuts[0])
    for cut in cuts[1:]:
        level = level * one(*cut)
    return level


def noise(key, dims, deviation, bound, cuts=(), held_as=jnp.bfloat16):
    level = block_scale(key, dims, cuts, -0.22, 0.18) if cuts else 1.0
    array = jax.random.normal(key, dims, jnp.float32) * deviation * level
    return jnp.minimum(jnp.maximum(array, -bound), bound).astype(held_as)


def setup_inputs(seed: int = 0, part: int = 0) -> dict:
    key_list = jax.random.split(jax.random.key(seed), 7)
    part_splits = jax.random.split(jax.random.fold_in(key_list[6], part), 7)
    return {
        "tokens": draw_tokens(jax.random.fold_in(jax.random.fold_in(key_list[6], part), 71), part),
        "w_query": noise(key_list[1], (D, HD), D ** -0.5, 0.09375, ((1, 2),)),
        "w_out": noise(key_list[2], (HD, D), (HD // 16) ** -0.5, 0.5, ((0, 2),)),
        "neighbour_kv": draw_neighbour_kv(jax.random.fold_in(jax.random.fold_in(key_list[6], part), 71), part),
        "shard_lists": draw_shard_lists(jax.random.fold_in(jax.random.fold_in(key_list[6], part), 71), part),
        "slot_lists": set_ends(jax.random.randint(part_splits[5], (OWNERS, OWN_BLOCKS, KN), 0, STORE_DEV), jax.random.fold_in(part_splits[5], 1), 0, STORE_DEV - 1).astype(jnp.int32),
    }


def reference(tokens, w_query, w_out, neighbour_kv, shard_lists, slot_lists):
    widened = tokens.astype(jnp.float32).reshape(SEQS * L, D)
    normed = (widened * lax.rsqrt(lax.optimization_barrier(jnp.mean(widened * widened, axis=1, keepdims=True)) + 1e-06)).astype(jnp.bfloat16)
    queries = (jnp.dot(normed, w_query, preferred_element_type=jnp.float32) * DH ** (-0.5)).astype(jnp.bfloat16)
    shards = shard_lists.reshape(N_SEQ, N_REP, SEQ_REP, SHARD_BLOCKS, KN)
    slot_ids = slot_lists.reshape(N_SEQ, N_REP, SEQ_REP, SHARD_BLOCKS, KN)
    replica = jnp.arange(N_REP, dtype=jnp.int32).reshape(1, N_REP, 1, 1, 1)
    store_rows = (shards * N_REP + replica) * STORE_DEV + slot_ids
    store_rows = jnp.transpose(store_rows, (1, 2, 0, 3, 4)).reshape(SEQS * (L // BLOCK), KN).astype(jnp.int32)
    query_blocks = queries.reshape(SEQS * (L // BLOCK), BLOCK, HEADS, DH)

    def attend(operands):
        picked, block_query = operands
        gathered = neighbour_kv[picked]
        key_rows = gathered[:, 0].reshape(KN * NLEN, HEADS, DH).astype(jnp.float32)
        value_rows = gathered[:, 1].reshape(KN * NLEN, HEADS, DH).astype(jnp.float32)
        scores = jnp.einsum('qhd,khd->hqk', block_query.astype(jnp.float32), key_rows)
        weights = jax.nn.softmax(scores, axis=-1).astype(jnp.bfloat16)
        weights = lax.optimization_barrier(weights)
        context = jnp.einsum('hqk,khd->qhd', weights.astype(jnp.float32), value_rows)
        return context.astype(jnp.bfloat16).reshape(BLOCK, HD)
    context = lax.map(attend, (store_rows, query_blocks)).reshape(SEQS * L, HD)
    group_width = HD // N_HEAD
    summed = jnp.zeros((SEQS * L, D), jnp.float32)
    for group_index in range(N_HEAD):
        lower = group_index * group_width
        term = jnp.dot(context[:, lower:lower + group_width], w_out[lower:lower + group_width], preferred_element_type=jnp.float32)
        rounded = lax.optimization_barrier(term.astype(jnp.bfloat16))
        summed = summed + rounded.astype(jnp.float32)
    return summed.astype(jnp.bfloat16).reshape(SEQS, L, D)
```

```python
import functools

import jax
import jax.numpy as jnp
from jax import lax
from jax.experimental import pallas as pl
from jax.experimental.pallas import tpu as pltpu
from jax.sharding import PartitionSpec as P

DH = 128
BLOCK = 64
KN = 2


def plain_body(tokens, w_query, w_out, neighbour_kv, shard_lists, slot_lists):
    local_seqs, local_span, feature_count = tokens.shape
    local_heads = w_query.shape[1] // DH
    widened = tokens.astype(jnp.float32)
    normed = (
        widened * lax.rsqrt(jnp.mean(widened * widened, axis=2, keepdims=True) + 1e-06)
    ).astype(jnp.bfloat16)
    product = jnp.einsum(
        "std,dh->sth",
        lax.all_gather(normed, "head", axis=0, tiled=True),
        w_query,
        preferred_element_type=jnp.float32,
    )
    queries = (product * DH ** (-0.5)).astype(jnp.bfloat16)
    seq_rep = queries.shape[0]
    own_blocks = seq_rep * local_span // BLOCK
    queries = queries.reshape(own_blocks, BLOCK, local_heads, DH)
    store_count = neighbour_kv.shape[0]
    row_shape = neighbour_kv.shape[1:]
    wanted = shard_lists[0] * store_count + slot_lists[0]
    pieces = lax.all_gather(neighbour_kv, "seq", axis=0, tiled=True)
    fetched = jnp.take(pieces, wanted.reshape(-1), axis=0).reshape((own_blocks, KN) + row_shape)
    key_rows = fetched[:, :, 0].reshape(own_blocks, KN * row_shape[1], local_heads, DH)
    value_rows = fetched[:, :, 1].reshape(own_blocks, KN * row_shape[1], local_heads, DH)
    scores = jnp.einsum("oqhd,okhd->ohqk", queries, key_rows, preferred_element_type=jnp.float32)
    weights = jax.nn.softmax(scores, axis=-1).astype(jnp.bfloat16)
    context = jnp.einsum(
        "ohqk,okhd->oqhd", weights, value_rows, preferred_element_type=jnp.float32
    ).astype(jnp.bfloat16)
    context = context.reshape(seq_rep, local_span, local_heads * DH)
    return lax.psum_scatter(
        jnp.einsum("sth,hd->std", context, w_out, preferred_element_type=jnp.float32).astype(
            jnp.bfloat16
        ),
        "head",
        scatter_dimension=0,
        tiled=True,
    )


def attend_kernel(n_kv, n_q, picks_ref, *refs):
    kv_refs = refs[:n_kv]
    q_refs = refs[n_kv:n_kv + n_q]
    o_refs = refs[n_kv + n_q:n_kv + 2 * n_q]
    store, sems = refs[n_kv + 2 * n_q:]
    count = kv_refs[0].shape[0]
    copies = [
        pltpu.make_async_copy(kv_refs[k], store.at[pl.ds(k * count, count)], sems.at[k])
        for k in range(n_kv)
    ]
    for copy in copies:
        copy.start()
    for copy in copies:
        copy.wait()
    rows, width = q_refs[0].shape
    blocks = rows // BLOCK
    heads = width // DH
    blank = jnp.zeros((BLOCK, DH), jnp.bfloat16)

    for piece in range(n_q):
        q_ref, o_ref = q_refs[piece], o_refs[piece]

        def step(block, carry, q_ref=q_ref, o_ref=o_ref, piece=piece):
            at = (piece * blocks + block) * KN
            chosen = [picks_ref[at + k] for k in range(KN)]
            keys = jnp.concatenate([store[i, 0] for i in chosen], axis=0)
            values = jnp.concatenate([store[i, 1] for i in chosen], axis=0)
            span = pl.ds(pl.multiple_of(block * BLOCK, BLOCK), BLOCK)
            q = q_ref[span, :]
            spread = jnp.concatenate(
                [
                    jnp.concatenate(
                        [q[:, h * DH:(h + 1) * DH] if h == g else blank for h in range(heads)], axis=1
                    )
                    for g in range(heads)
                ],
                axis=0,
            )
            scores = lax.dot_general(
                spread, keys, (((1,), (1,)), ((), ())), preferred_element_type=jnp.float32
            )
            grown = jnp.exp(scores - jnp.max(scores, axis=-1, keepdims=True))
            weights = (grown / jnp.sum(grown, axis=-1, keepdims=True)).astype(jnp.bfloat16)
            mixed = jnp.dot(weights, values, preferred_element_type=jnp.float32)
            o_ref[span, :] = jnp.concatenate(
                [mixed[h * BLOCK:(h + 1) * BLOCK, h * DH:(h + 1) * DH] for h in range(heads)], axis=1
            ).astype(jnp.bfloat16)
            return carry

        lax.fori_loop(0, blocks, step, 0, unroll=4 if blocks % 4 == 0 else 1)


def attend(picks, kv_pieces, q_pieces):
    n_kv, n_q = len(kv_pieces), len(q_pieces)
    count = kv_pieces[0].shape[0]
    whole = pl.BlockSpec(memory_space=pltpu.VMEM)
    return pl.pallas_call(
        functools.partial(attend_kernel, n_kv, n_q),
        out_shape=[jax.ShapeDtypeStruct(q.shape, q.dtype) for q in q_pieces],
        in_specs=[pl.BlockSpec(memory_space=pltpu.SMEM)]
        + [pl.BlockSpec(memory_space=pl.ANY)] * n_kv
        + [whole] * n_q,
        out_specs=[whole] * n_q,
        scratch_shapes=[
            pltpu.VMEM((n_kv * count,) + kv_pieces[0].shape[1:], jnp.bfloat16),
            pltpu.SemaphoreType.DMA((n_kv,)),
        ],
        compiler_params=pltpu.CompilerParams(vmem_limit_bytes=48 * 2**20),
        name="attend",
    )(picks, *kv_pieces, *q_pieces)


def spread_body(n_seq, n_head, tokens, w_query, w_out, neighbour_kv, shard_lists, slot_lists):
    s = lax.axis_index("seq")
    x = lax.axis_index("head")
    r = lax.axis_index("rep")
    local_seqs, local_span, features = tokens.shape
    rows = local_seqs * local_span
    local_width = w_query.shape[1]
    width = local_width // n_seq
    store_count = neighbour_kv.shape[0]
    flip = [(0, 1), (1, 0)]

    def send(array, dz, dx):
        order = []
        for a in range(n_seq):
            for b in range(n_head):
                order.append((a * n_head + b, (a + dz) % n_seq * n_head + (b + dx) % n_head))
        return lax.ppermute(array, ("seq", "head"), order)

    def columns(array, dz):
        at = lax.rem(s + dz, n_seq) * width
        return lax.dynamic_slice_in_dim(array, at, width, axis=array.ndim - 1)

    def other_half(w, axis):
        half = w.shape[axis] // 2
        mine = lax.dynamic_slice_in_dim(w, r * half, half, axis=axis)
        first = lax.ppermute(mine, "head", flip)
        second = lax.ppermute(first, "rep", flip)
        low = jnp.where(r == 0, first, second)
        high = jnp.where(r == 0, second, first)
        return jnp.concatenate([low, high], axis=axis)

    kv_pieces = [columns(neighbour_kv, 0)]
    for dz in range(1, n_seq):
        kv_pieces.append(send(columns(neighbour_kv, dz), dz, 0))

    w_query_other = other_half(w_query, 0)
    w_out_other = other_half(w_out, 0)

    lists = jnp.stack([shard_lists[0], slot_lists[0]])
    gathered = lax.all_gather(lists, "seq", axis=0)
    places = lax.rem(s - gathered[:, 0] + n_seq, n_seq) * store_count + gathered[:, 1]
    places = places.reshape(n_seq, n_head, -1)
    picks = []
    for dz in range(n_seq):
        for dx in range(n_head):
            picks.append(places[lax.rem(s - dz + n_seq, n_seq), lax.rem(x - dx + n_head, n_head)])
    picks = jnp.concatenate(picks).astype(jnp.int32)

    widened = tokens.reshape(rows, features).astype(jnp.float32)
    normed = (
        widened * lax.rsqrt(jnp.mean(widened * widened, axis=1, keepdims=True) + 1e-06)
    ).astype(jnp.bfloat16)

    def project(w):
        product = jnp.dot(normed, w, preferred_element_type=jnp.float32)
        return (product * DH ** (-0.5)).astype(jnp.bfloat16)

    queries = [project(w_query), project(w_query_other)]
    q_pieces = []
    for dz in range(n_seq):
        for dx in range(n_head):
            piece = columns(queries[dx], dz)
            q_pieces.append(piece if dz == dx == 0 else send(piece, dz, dx))

    c_pieces = attend(picks, kv_pieces, q_pieces)

    back = [[None] * n_seq for _ in range(n_head)]
    for dz in range(n_seq):
        for dx in range(n_head):
            piece = c_pieces[dz * n_head + dx]
            back[dx][dz] = piece if dz == dx == 0 else send(piece, -dz, -dx)
    terms = []
    for dx, w in enumerate([w_out, w_out_other]):
        twice = jnp.concatenate(back[dx] + back[dx], axis=1)
        context = lax.dynamic_slice_in_dim(
            twice, lax.rem(n_seq - s, n_seq) * width, local_width, axis=1
        )
        terms.append(jnp.dot(context, w, preferred_element_type=jnp.float32).astype(jnp.bfloat16))
    crossed = (terms[0].astype(jnp.float32) + terms[1].astype(jnp.float32)).astype(jnp.bfloat16)
    return crossed.reshape(local_seqs, local_span, w_out.shape[1])


def solution(mesh):
    placed = (
        P(("grp", "rep", "head"), "seq", None),
        P(None, "head"),
        P("head", None),
        P(("grp", "seq", "rep"), None, None, "head"),
        P(("grp", "seq", "rep"), None, None),
        P(("grp", "seq", "rep"), None, None),
    )
    sizes = dict(mesh.shape)
    n_seq, n_head = sizes["seq"], sizes["head"]

    def body(*arrays):
        local_heads = arrays[1].shape[1] // DH
        if n_head == 2 and sizes["rep"] == 2 and local_heads % n_seq == 0:
            return spread_body(n_seq, n_head, *arrays)
        return plain_body(*arrays)

    return jax.shard_map(
        body,
        mesh=mesh,
        in_specs=placed,
        out_specs=P(("grp", "rep", "head"), "seq", None),
        check_vma=False,
    )
```

```python
import functools

import jax
import jax.numpy as jnp
from jax import lax
from jax.experimental import pallas as pl
from jax.experimental.pallas import tpu as pltpu
from jax.sharding import PartitionSpec as P

DH = 128
BLOCK = 64
KN = 2


def plain_body(tokens, w_query, w_out, neighbour_kv, shard_lists, slot_lists):
    local_seqs, local_span, feature_count = tokens.shape
    local_heads = w_query.shape[1] // DH
    widened = tokens.astype(jnp.float32)
    normed = (
        widened * lax.rsqrt(jnp.mean(widened * widened, axis=2, keepdims=True) + 1e-06)
    ).astype(jnp.bfloat16)
    product = jnp.einsum(
        "std,dh->sth",
        lax.all_gather(normed, "head", axis=0, tiled=True),
        w_query,
        preferred_element_type=jnp.float32,
    )
    queries = (product * DH ** (-0.5)).astype(jnp.bfloat16)
    seq_rep = queries.shape[0]
    own_blocks = seq_rep * local_span // BLOCK
    queries = queries.reshape(own_blocks, BLOCK, local_heads, DH)
    store_count = neighbour_kv.shape[0]
    row_shape = neighbour_kv.shape[1:]
    wanted = shard_lists[0] * store_count + slot_lists[0]
    pieces = lax.all_gather(neighbour_kv, "seq", axis=0, tiled=True)
    fetched = jnp.take(pieces, wanted.reshape(-1), axis=0).reshape((own_blocks, KN) + row_shape)
    key_rows = fetched[:, :, 0].reshape(own_blocks, KN * row_shape[1], local_heads, DH)
    value_rows = fetched[:, :, 1].reshape(own_blocks, KN * row_shape[1], local_heads, DH)
    scores = jnp.einsum("oqhd,okhd->ohqk", queries, key_rows, preferred_element_type=jnp.float32)
    weights = jax.nn.softmax(scores, axis=-1).astype(jnp.bfloat16)
    context = jnp.einsum(
        "ohqk,okhd->oqhd", weights, value_rows, preferred_element_type=jnp.float32
    ).astype(jnp.bfloat16)
    context = context.reshape(seq_rep, local_span, local_heads * DH)
    return lax.psum_scatter(
        jnp.einsum("sth,hd->std", context, w_out, preferred_element_type=jnp.float32).astype(
            jnp.bfloat16
        ),
        "head",
        scatter_dimension=0,
        tiled=True,
    )


MESH = pl.DeviceIdType.MESH
ROW_TILE = 512
NORM_TILE = 32


def flow_kernel(
    n_seq, n_head, tokens, w_query, w_out, kv, lists,
    context, w_out_other,
    store, q_in, q_out, c_out, normed, wq_own, wq_other, lists_in, picks,
    kv_send, kv_recv, q_send, q_recv, c_send, c_recv, w_send, w_recv, l_send, l_recv, local, token_sem,
):
    s = lax.axis_index("seq")
    x = lax.axis_index("head")
    r = lax.axis_index("rep")
    rows, features = tokens.shape
    count = kv.shape[0]
    width = q_in.shape[2]
    heads = width // DH
    blocks = rows // BLOCK
    pieces = n_seq * n_head

    def peer(dz, dx):
        return {
            "seq": lax.rem(s + dz + n_seq, n_seq),
            "head": lax.rem(x + dx + n_head, n_head),
        }

    def cols(index):
        return pl.ds(pl.multiple_of(index * width, width), width)

    def remote(src, dst, send, recv, device):
        return pltpu.make_async_remote_copy(
            src_ref=src, dst_ref=dst, send_sem=send, recv_sem=recv, device_id=device, device_id_type=MESH
        )

    barrier = pltpu.get_barrier_semaphore()
    for p in range(1, pieces):
        pl.semaphore_signal(barrier, inc=1, device_id=peer(p // n_head, p % n_head), device_id_type=MESH)
    pl.semaphore_signal(barrier, inc=1, device_id={"rep": 1 - r}, device_id_type=MESH)
    pl.semaphore_wait(barrier, pieces)

    def kv_copy(dz):
        to = lax.rem(s + dz, n_seq)
        return remote(
            kv.at[:, :, :, cols(to)], store.at[pl.ds(s * count, count)],
            kv_send.at[dz], kv_recv.at[dz], peer(dz, 0),
        )

    def list_copy(dz):
        return remote(lists, lists_in.at[dz], l_send.at[dz], l_recv.at[dz], peer(dz, 0))

    def q_copy(p):
        return remote(
            q_out.at[p], q_in.at[p], q_send.at[p], q_recv.at[p], peer(p // n_head, p % n_head)
        )

    def c_copy(p):
        dz, dx = p // n_head, p % n_head
        return remote(
            c_out.at[p], context.at[dx, :, cols(s)], c_send.at[p], c_recv.at[p], peer(-dz, -dx)
        )

    half = features // 2
    wq_rows = pl.ds(pl.multiple_of(r * half, half), half)
    wq_x = remote(w_query.at[wq_rows], wq_other.at[wq_rows], w_send.at[0], w_recv.at[0], peer(0, 1))
    wq_c = remote(
        wq_other.at[wq_rows], wq_other.at[wq_rows], w_send.at[1], w_recv.at[1], {"rep": 1 - r}
    )
    wo_half = w_out.shape[0] // 2
    wo_rows = pl.ds(pl.multiple_of(r * wo_half, wo_half), wo_half)
    wo_x = remote(w_out.at[wo_rows], w_out_other.at[wo_rows], w_send.at[2], w_recv.at[2], peer(0, 1))
    wo_c = remote(
        w_out_other.at[wo_rows], w_out_other.at[wo_rows], w_send.at[3], w_recv.at[3], {"rep": 1 - r}
    )

    tiles = 4
    tile_rows = rows // tiles
    token_copies = [
        pltpu.make_async_copy(
            tokens.at[pl.ds(t * tile_rows, tile_rows)], normed.at[pl.ds(t * tile_rows, tile_rows)],
            token_sem.at[t],
        )
        for t in range(tiles)
    ]
    wq_local = pltpu.make_async_copy(w_query, wq_own, local.at[0])
    kv_local = pltpu.make_async_copy(
        kv.at[:, :, :, cols(s)], store.at[pl.ds(s * count, count)], local.at[1]
    )
    list_local = pltpu.make_async_copy(lists, lists_in.at[0], local.at[2])

    wq_x.start()
    for copy in token_copies:
        copy.start()
    for dz in range(1, n_seq):
        list_copy(dz).start()
    for dz in range(1, n_seq):
        kv_copy(dz).start()
    wq_local.start()
    list_local.start()
    kv_local.start()

    def norm(t, carry):
        span = pl.ds(pl.multiple_of(t * NORM_TILE, NORM_TILE), NORM_TILE)
        wide = normed[span, :].astype(jnp.float32)
        scale = lax.rsqrt(jnp.mean(wide * wide, axis=1, keepdims=True) + 1e-06)
        normed[span, :] = (wide * scale).astype(jnp.bfloat16)
        return carry

    per_tile = tile_rows // NORM_TILE
    for t in range(tiles):
        token_copies[t].wait()
        lax.fori_loop(t * per_tile, (t + 1) * per_tile, norm, 0)

    def project(w, to, dst):
        def tile(t, carry):
            span = pl.ds(pl.multiple_of(t * ROW_TILE, ROW_TILE), ROW_TILE)
            product = jnp.dot(normed[span, :], w[:, cols(to)], preferred_element_type=jnp.float32)
            dst[span, :] = (product * DH ** (-0.5)).astype(jnp.bfloat16)
            return carry

        lax.fori_loop(0, rows // ROW_TILE, tile, 0)

    def project_send(w, dx, first):
        def one(dz, carry):
            p = dz * n_head + dx
            project(w, lax.rem(s + dz, n_seq), q_out.at[p])
            q_copy(p).start()
            return carry

        lax.fori_loop(first, n_seq, one, 0)

    wq_local.wait()
    project_send(wq_own, 0, 1)
    wq_x.wait_recv()
    wq_c.start()
    project(wq_own, s, q_in.at[0])
    wq_c.wait_recv()
    project_send(wq_other, 1, 0)
    wo_x.start()

    list_local.wait()
    for dz in range(1, n_seq):
        list_copy(dz).wait_recv()
    picks_copy = pltpu.make_async_copy(lists_in, picks, local.at[3])
    picks_copy.start()
    picks_copy.wait()
    kv_local.wait()
    for dz in range(1, n_seq):
        kv_copy(dz).wait_recv()
    wo_x.wait_recv()
    wo_c.start()

    blank = jnp.zeros((BLOCK, DH), jnp.bfloat16)

    def attend(p):
        dz, dx = p // n_head, p % n_head
        base = lax.rem(x - dx + n_head, n_head) * blocks

        def step(block, carry):
            at = (base + block) * KN
            chosen = [picks[dz, 0, at + k] for k in range(KN)]
            keys = jnp.concatenate([store[i, 0] for i in chosen], axis=0)
            values = jnp.concatenate([store[i, 1] for i in chosen], axis=0)
            span = pl.ds(pl.multiple_of(block * BLOCK, BLOCK), BLOCK)
            q = q_in[p, span, :]
            spread = jnp.concatenate(
                [
                    jnp.concatenate(
                        [q[:, h * DH:(h + 1) * DH] if h == g else blank for h in range(heads)], axis=1
                    )
                    for g in range(heads)
                ],
                axis=0,
            )
            scores = lax.dot_general(
                spread, keys, (((1,), (1,)), ((), ())), preferred_element_type=jnp.float32
            )
            grown = jnp.exp(scores - jnp.max(scores, axis=-1, keepdims=True))
            weights = (grown / jnp.sum(grown, axis=-1, keepdims=True)).astype(jnp.bfloat16)
            mixed = jnp.dot(weights, values, preferred_element_type=jnp.float32)
            c_out[p, span, :] = jnp.concatenate(
                [mixed[h * BLOCK:(h + 1) * BLOCK, h * DH:(h + 1) * DH] for h in range(heads)], axis=1
            ).astype(jnp.bfloat16)
            return carry

        lax.fori_loop(0, blocks, step, 0, unroll=4 if blocks % 4 == 0 else 1)

    def remote_piece(t, carry):
        p = lax.rem(t // n_head + 1, n_seq) * n_head + (n_head - 1 - lax.rem(t, n_head))
        q_copy(p).wait_recv()
        attend(p)
        c_copy(p).start()
        return carry

    lax.fori_loop(0, pieces - 1, remote_piece, 0)
    attend(0)
    own = pltpu.make_async_copy(c_out.at[0], context.at[0, :, cols(s)], local.at[4])
    own.start()

    for dz in range(1, n_seq):
        kv_copy(dz).wait_send()
        list_copy(dz).wait_send()
    for copy in (wq_x, wq_c, wo_x, wo_c):
        copy.wait_send()
    wo_c.wait_recv()
    for p in range(1, pieces):
        q_copy(p).wait_send()
    for p in range(1, pieces):
        c_copy(p).wait_send()
        c_copy(p).wait_recv()
    own.wait()


def spread_body(n_seq, n_head, tokens, w_query, w_out, neighbour_kv, shard_lists, slot_lists):
    local_seqs, local_span, features = tokens.shape
    rows = local_seqs * local_span
    local_width = w_query.shape[1]
    width = local_width // n_seq
    count, _, length, _ = neighbour_kv.shape
    pieces = n_seq * n_head
    places = (shard_lists[0] * count + slot_lists[0]).reshape(1, -1).astype(jnp.int32)
    lanes = -(-places.shape[1] // 128) * 128
    places = jnp.pad(places, ((0, 7), (0, lanes - places.shape[1])))
    bf16 = jnp.bfloat16
    anywhere = pl.BlockSpec(memory_space=pl.ANY)
    dma = pltpu.SemaphoreType.DMA
    context, w_out_other = pl.pallas_call(
        functools.partial(flow_kernel, n_seq, n_head),
        out_shape=[
            jax.ShapeDtypeStruct((n_head, rows, local_width), bf16),
            jax.ShapeDtypeStruct(w_out.shape, bf16),
        ],
        in_specs=[anywhere] * 4 + [pl.BlockSpec(memory_space=pltpu.VMEM)],
        out_specs=[anywhere] * 2,
        scratch_shapes=[
            pltpu.VMEM((n_seq * count, 2, length, width), bf16),
            pltpu.VMEM((pieces, rows, width), bf16),
            pltpu.VMEM((pieces, rows, width), bf16),
            pltpu.VMEM((pieces, rows, width), bf16),
            pltpu.VMEM((rows, features), bf16),
            pltpu.VMEM((features, local_width), bf16),
            pltpu.VMEM((features, local_width), bf16),
            pltpu.VMEM((n_seq, 8, lanes), jnp.int32),
            pltpu.SMEM((n_seq, 8, lanes), jnp.int32),
            dma((n_seq,)), dma((n_seq,)),
            dma((pieces,)), dma((pieces,)),
            dma((pieces,)), dma((pieces,)),
            dma((4,)), dma((4,)),
            dma((n_seq,)), dma((n_seq,)),
            dma((5,)), dma((4,)),
        ],
        compiler_params=pltpu.CompilerParams(
            collective_id=0, has_side_effects=True, vmem_limit_bytes=58 * 2**20
        ),
        cost_estimate=pl.CostEstimate(
            flops=2 * rows * features * local_width * n_head, bytes_accessed=2**26, transcendentals=2**22
        ),
        name="flow",
    )(tokens.reshape(rows, features), w_query, w_out, neighbour_kv, places)
    terms = [
        lax.reduce_precision(
            jnp.dot(context[dx], w, preferred_element_type=jnp.float32), exponent_bits=8, mantissa_bits=7
        )
        for dx, w in enumerate([w_out, w_out_other])
    ]
    return (terms[0] + terms[1]).astype(bf16).reshape(local_seqs, local_span, w_out.shape[1])


def solution(mesh):
    placed = (
        P(("grp", "rep", "head"), "seq", None),
        P(None, "head"),
        P("head", None),
        P(("grp", "seq", "rep"), None, None, "head"),
        P(("grp", "seq", "rep"), None, None),
        P(("grp", "seq", "rep"), None, None),
    )
    sizes = dict(mesh.shape)
    n_seq, n_head = sizes["seq"], sizes["head"]

    def body(*arrays):
        local_heads = arrays[1].shape[1] // DH
        if n_head == 2 and sizes["rep"] == 2 and local_heads % n_seq == 0:
            return spread_body(n_seq, n_head, *arrays)
        return plain_body(*arrays)

    return jax.shard_map(
        body,
        mesh=mesh,
        in_specs=placed,
        out_specs=P(("grp", "rep", "head"), "seq", None),
        check_vma=False,
    )
```

```python
import functools

import jax
import jax.numpy as jnp
from jax import lax
from jax.experimental import pallas as pl
from jax.experimental.pallas import tpu as pltpu
from jax.sharding import PartitionSpec as P

DH = 128
BLOCK = 64
KN = 2


def plain_body(tokens, w_query, w_out, neighbour_kv, shard_lists, slot_lists):
    local_seqs, local_span, feature_count = tokens.shape
    local_heads = w_query.shape[1] // DH
    widened = tokens.astype(jnp.float32)
    normed = (
        widened * lax.rsqrt(jnp.mean(widened * widened, axis=2, keepdims=True) + 1e-06)
    ).astype(jnp.bfloat16)
    product = jnp.einsum(
        "std,dh->sth",
        lax.all_gather(normed, "head", axis=0, tiled=True),
        w_query,
        preferred_element_type=jnp.float32,
    )
    queries = (product * DH ** (-0.5)).astype(jnp.bfloat16)
    seq_rep = queries.shape[0]
    own_blocks = seq_rep * local_span // BLOCK
    queries = queries.reshape(own_blocks, BLOCK, local_heads, DH)
    store_count = neighbour_kv.shape[0]
    row_shape = neighbour_kv.shape[1:]
    wanted = shard_lists[0] * store_count + slot_lists[0]
    pieces = lax.all_gather(neighbour_kv, "seq", axis=0, tiled=True)
    fetched = jnp.take(pieces, wanted.reshape(-1), axis=0).reshape((own_blocks, KN) + row_shape)
    key_rows = fetched[:, :, 0].reshape(own_blocks, KN * row_shape[1], local_heads, DH)
    value_rows = fetched[:, :, 1].reshape(own_blocks, KN * row_shape[1], local_heads, DH)
    scores = jnp.einsum("oqhd,okhd->ohqk", queries, key_rows, preferred_element_type=jnp.float32)
    weights = jax.nn.softmax(scores, axis=-1).astype(jnp.bfloat16)
    context = jnp.einsum(
        "ohqk,okhd->oqhd", weights, value_rows, preferred_element_type=jnp.float32
    ).astype(jnp.bfloat16)
    context = context.reshape(seq_rep, local_span, local_heads * DH)
    return lax.psum_scatter(
        jnp.einsum("sth,hd->std", context, w_out, preferred_element_type=jnp.float32).astype(
            jnp.bfloat16
        ),
        "head",
        scatter_dimension=0,
        tiled=True,
    )


MESH = pl.DeviceIdType.MESH
ROW_TILE = 512
CHUNKS = 4
LAG = 2
NORM_TILE = 32


def flow_kernel(
    n_seq, n_head, tokens, w_query, w_out, kv, lists,
    crossed, w_out_other,
    context, store, q_in, q_out, c_out, normed, wq_own, wq_other, lists_in, picks,
    kv_send, kv_recv, q_send, q_recv, c_send, c_recv, w_send, w_recv, l_send, l_recv, local, token_sem,
    own_sem, out_sem, load_sem,
):
    s = lax.axis_index("seq")
    x = lax.axis_index("head")
    r = lax.axis_index("rep")
    rows, features = tokens.shape
    count = kv.shape[0]
    width = q_in.shape[2]
    heads = width // DH
    blocks = rows // BLOCK
    pieces = n_seq * n_head

    def peer(dz, dx):
        return {
            "seq": lax.rem(s + dz + n_seq, n_seq),
            "head": lax.rem(x + dx + n_head, n_head),
        }

    def cols(index):
        return pl.ds(pl.multiple_of(index * width, width), width)

    def remote(src, dst, send, recv, device):
        return pltpu.make_async_remote_copy(
            src_ref=src, dst_ref=dst, send_sem=send, recv_sem=recv, device_id=device, device_id_type=MESH
        )

    barrier = pltpu.get_barrier_semaphore()
    for p in range(1, pieces):
        pl.semaphore_signal(barrier, inc=1, device_id=peer(p // n_head, p % n_head), device_id_type=MESH)
    pl.semaphore_signal(barrier, inc=1, device_id={"rep": 1 - r}, device_id_type=MESH)
    pl.semaphore_wait(barrier, pieces)

    def kv_copy(dz):
        to = lax.rem(s + dz, n_seq)
        return remote(
            kv.at[:, :, :, cols(to)], store.at[pl.ds(s * count, count)],
            kv_send.at[dz], kv_recv.at[dz], peer(dz, 0),
        )

    def list_copy(dz):
        return remote(lists, lists_in.at[dz], l_send.at[dz], l_recv.at[dz], peer(dz, 0))

    chunk_rows = rows // CHUNKS
    chunk_blocks = blocks // CHUNKS

    def chunk_span(c):
        return pl.ds(pl.multiple_of(c * chunk_rows, chunk_rows), chunk_rows)

    def q_copy(p, c):
        span = chunk_span(c)
        return remote(
            q_out.at[p, span], q_in.at[p, span], q_send.at[p, c], q_recv.at[p, c],
            peer(p // n_head, p % n_head),
        )

    def c_copy(p, c):
        dz, dx = p // n_head, p % n_head
        span = chunk_span(c)
        return remote(
            c_out.at[p, span], context.at[dx, span, cols(s)], c_send.at[p, c], c_recv.at[p, c],
            peer(-dz, -dx),
        )

    def own_copy(c):
        span = chunk_span(c)
        return pltpu.make_async_copy(
            c_out.at[0, span], context.at[0, span, cols(s)], own_sem.at[c]
        )

    def out_copy(c):
        span = chunk_span(c)
        return pltpu.make_async_copy(normed.at[span], crossed.at[span], out_sem.at[c])

    local_width = w_out.shape[0]
    out_tiles = features // local_width

    def w_load(source, target, which, t):
        return pltpu.make_async_copy(
            source.at[:, pl.ds(t * local_width, local_width)],
            target.at[pl.ds(t * local_width, local_width)],
            load_sem.at[which, t],
        )

    def far_piece(u):
        dz = lax.rem(u // n_head + n_seq // 2 - 1, n_seq - 1) + 1
        return dz * n_head + (n_head - 1 - lax.rem(u, n_head))

    far = (n_seq - 1) * n_head
    far_order = [(t + n_seq // 2 - 1) % (n_seq - 1) + 1 for t in range(n_seq - 1)]

    half = features // 2
    wq_rows = pl.ds(pl.multiple_of(r * half, half), half)
    wq_x = remote(w_query.at[wq_rows], wq_other.at[wq_rows], w_send.at[0], w_recv.at[0], peer(0, 1))
    wq_c = remote(
        wq_other.at[wq_rows], wq_other.at[wq_rows], w_send.at[1], w_recv.at[1], {"rep": 1 - r}
    )
    wo_half = w_out.shape[0] // 2
    wo_rows = pl.ds(pl.multiple_of(r * wo_half, wo_half), wo_half)
    wo_x = remote(w_out.at[wo_rows], w_out_other.at[wo_rows], w_send.at[2], w_recv.at[2], peer(0, 1))
    wo_c = remote(
        w_out_other.at[wo_rows], w_out_other.at[wo_rows], w_send.at[3], w_recv.at[3], {"rep": 1 - r}
    )

    tiles = 4
    tile_rows = rows // tiles
    token_copies = [
        pltpu.make_async_copy(
            tokens.at[pl.ds(t * tile_rows, tile_rows)], normed.at[pl.ds(t * tile_rows, tile_rows)],
            token_sem.at[t],
        )
        for t in range(tiles)
    ]
    wq_local = pltpu.make_async_copy(w_query, wq_own, local.at[0])
    kv_local = pltpu.make_async_copy(
        kv.at[:, :, :, cols(s)], store.at[pl.ds(s * count, count)], local.at[1]
    )
    list_local = pltpu.make_async_copy(lists, lists_in.at[0], local.at[2])

    wq_x.start()
    for copy in token_copies:
        copy.start()
    for dz in range(1, n_seq):
        list_copy(dz).start()
    for dz in far_order:
        kv_copy(dz).start()
    wq_local.start()
    list_local.start()
    kv_local.start()

    def norm(t, carry):
        span = pl.ds(pl.multiple_of(t * NORM_TILE, NORM_TILE), NORM_TILE)
        wide = normed[span, :].astype(jnp.float32)
        scale = lax.rsqrt(jnp.mean(wide * wide, axis=1, keepdims=True) + 1e-06)
        normed[span, :] = (wide * scale).astype(jnp.bfloat16)
        return carry

    per_tile = tile_rows // NORM_TILE
    for t in range(tiles):
        token_copies[t].wait()
        lax.fori_loop(t * per_tile, (t + 1) * per_tile, norm, 0)

    def project(w, to, dst):
        def tile(t, carry):
            span = pl.ds(pl.multiple_of(t * ROW_TILE, ROW_TILE), ROW_TILE)
            product = jnp.dot(normed[span, :], w[:, cols(to)], preferred_element_type=jnp.float32)
            dst[span, :] = (product * DH ** (-0.5)).astype(jnp.bfloat16)
            return carry

        lax.fori_loop(0, rows // ROW_TILE, tile, 0)

    def project_all(w, dx, first):
        def one(dz, carry):
            project(w, lax.rem(s + dz, n_seq), q_out.at[dz * n_head + dx])
            return carry

        lax.fori_loop(first, n_seq, one, 0)

    wq_local.wait()
    project(wq_own, s, q_in.at[0])
    project_all(wq_own, 0, 1)
    for t in range(out_tiles):
        w_load(w_out, wq_own, 0, t).start()
    wq_x.wait_recv()
    wo_x.start()
    wq_c.start()
    wq_c.wait_recv()
    project_all(wq_other, 1, 0)
    for c in range(CHUNKS):
        q_copy(1, c).start()
    for dz in range(1, n_seq):
        kv_copy(dz).wait_send()

    def q_start(t, carry):
        q_copy(far_piece(lax.rem(t, far)), t // far).start()
        return carry

    lax.fori_loop(0, far * CHUNKS, q_start, 0)

    list_local.wait()
    for dz in range(1, n_seq):
        list_copy(dz).wait_recv()
    picks_copy = pltpu.make_async_copy(lists_in, picks, local.at[3])
    picks_copy.start()
    picks_copy.wait()
    kv_local.wait()
    for dz in range(1, n_seq):
        kv_copy(dz).wait_recv()
    wo_x.wait_recv()
    wo_c.start()
    wq_x.wait_send()
    wq_c.wait_send()

    blank = jnp.zeros((BLOCK, DH), jnp.bfloat16)

    def attend(p, c):
        dz, dx = p // n_head, p % n_head
        base = lax.rem(x - dx + n_head, n_head) * blocks

        def step(block, carry):
            block = c * chunk_blocks + block
            at = (base + block) * KN
            chosen = [picks[dz, 0, at + k] for k in range(KN)]
            keys = jnp.concatenate([store[i, 0] for i in chosen], axis=0)
            values = jnp.concatenate([store[i, 1] for i in chosen], axis=0)
            span = pl.ds(pl.multiple_of(block * BLOCK, BLOCK), BLOCK)
            q = q_in[p, span, :]
            spread = jnp.concatenate(
                [
                    jnp.concatenate(
                        [q[:, h * DH:(h + 1) * DH] if h == g else blank for h in range(heads)], axis=1
                    )
                    for g in range(heads)
                ],
                axis=0,
            )
            scores = lax.dot_general(
                spread, keys, (((1,), (1,)), ((), ())), preferred_element_type=jnp.float32
            )
            grown = jnp.exp(scores - jnp.max(scores, axis=-1, keepdims=True))
            weights = (grown / jnp.sum(grown, axis=-1, keepdims=True)).astype(jnp.bfloat16)
            mixed = jnp.dot(weights, values, preferred_element_type=jnp.float32)
            c_out[p, span, :] = jnp.concatenate(
                [mixed[h * BLOCK:(h + 1) * BLOCK, h * DH:(h + 1) * DH] for h in range(heads)], axis=1
            ).astype(jnp.bfloat16)
            return carry

        lax.fori_loop(0, chunk_blocks, step, 0, unroll=4 if chunk_blocks % 4 == 0 else 1)

    def output(c):
        span = chunk_span(c)
        own_copy(c).wait()
        for p in range(1, pieces):
            c_copy(p, c).wait_recv()

        def tile(t, carry):
            depth = pl.ds(pl.multiple_of(t * local_width, local_width), local_width)
            total = jnp.zeros((chunk_rows, local_width), jnp.float32)
            for dx, w in enumerate((wq_own, wq_other)):
                term = jnp.dot(context[dx, span, :], w[depth, :], preferred_element_type=jnp.float32)
                total = total + term.astype(jnp.bfloat16).astype(jnp.float32)
            normed[span, depth] = total.astype(jnp.bfloat16)
            return carry

        lax.fori_loop(0, out_tiles, tile, 0)
        out_copy(c).start()

    def turn(c, carry):
        @pl.when(c < CHUNKS)
        def _():
            attend(0, c)
            own_copy(c).start()

            def one(t, carry):
                p = jnp.where(t == 0, 1, far_piece(jnp.maximum(t - 1, 0)))
                q_copy(p, c).wait_recv()
                attend(p, c)
                c_copy(p, c).start()
                return carry

            lax.fori_loop(0, pieces - 1, one, 0)

        @pl.when(c == LAG)
        def _():
            wo_c.wait_recv()
            for t in range(out_tiles):
                w_load(w_out_other, wq_other, 1, t).start()
            for t in range(out_tiles):
                w_load(w_out, wq_own, 0, t).wait()
                w_load(w_out_other, wq_other, 1, t).wait()

        @pl.when(c >= LAG)
        def _():
            output(c - LAG)

        return carry

    lax.fori_loop(0, CHUNKS + LAG, turn, 0)

    for dz in range(1, n_seq):
        list_copy(dz).wait_send()
    for copy in (wo_x, wo_c):
        copy.wait_send()

    def drain(t, carry):
        p, c = t // CHUNKS + 1, lax.rem(t, CHUNKS)
        q_copy(p, c).wait_send()
        c_copy(p, c).wait_send()
        return carry

    lax.fori_loop(0, (pieces - 1) * CHUNKS, drain, 0)
    for c in range(CHUNKS):
        out_copy(c).wait()


def spread_body(n_seq, n_head, tokens, w_query, w_out, neighbour_kv, shard_lists, slot_lists):
    local_seqs, local_span, features = tokens.shape
    rows = local_seqs * local_span
    local_width = w_query.shape[1]
    width = local_width // n_seq
    count, _, length, _ = neighbour_kv.shape
    pieces = n_seq * n_head
    places = (shard_lists[0] * count + slot_lists[0]).reshape(1, -1).astype(jnp.int32)
    lanes = -(-places.shape[1] // 128) * 128
    places = jnp.pad(places, ((0, 7), (0, lanes - places.shape[1])))
    bf16 = jnp.bfloat16
    anywhere = pl.BlockSpec(memory_space=pl.ANY)
    dma = pltpu.SemaphoreType.DMA
    crossed, _ = pl.pallas_call(
        functools.partial(flow_kernel, n_seq, n_head),
        out_shape=[
            jax.ShapeDtypeStruct((rows, w_out.shape[1]), bf16),
            jax.ShapeDtypeStruct(w_out.shape, bf16),
        ],
        in_specs=[anywhere] * 4 + [pl.BlockSpec(memory_space=pltpu.VMEM)],
        out_specs=[anywhere] * 2,
        scratch_shapes=[
            pltpu.VMEM((n_head, rows, local_width), bf16),
            pltpu.VMEM((n_seq * count, 2, length, width), bf16),
            pltpu.VMEM((pieces, rows, width), bf16),
            pltpu.VMEM((pieces, rows, width), bf16),
            pltpu.VMEM((pieces, rows, width), bf16),
            pltpu.VMEM((rows, features), bf16),
            pltpu.VMEM((features, local_width), bf16),
            pltpu.VMEM((features, local_width), bf16),
            pltpu.VMEM((n_seq, 8, lanes), jnp.int32),
            pltpu.SMEM((n_seq, 8, lanes), jnp.int32),
            dma((n_seq,)), dma((n_seq,)),
            dma((pieces, CHUNKS)), dma((pieces, CHUNKS)),
            dma((pieces, CHUNKS)), dma((pieces, CHUNKS)),
            dma((4,)), dma((4,)),
            dma((n_seq,)), dma((n_seq,)),
            dma((4,)), dma((4,)),
            dma((CHUNKS,)), dma((CHUNKS,)), dma((2, features // local_width)),
        ],
        compiler_params=pltpu.CompilerParams(
            collective_id=0, has_side_effects=True, vmem_limit_bytes=58 * 2**20
        ),
        cost_estimate=pl.CostEstimate(
            flops=2 * rows * features * local_width * n_head, bytes_accessed=2**26, transcendentals=2**22
        ),
        name="flow",
    )(tokens.reshape(rows, features), w_query, w_out, neighbour_kv, places)
    return crossed.reshape(local_seqs, local_span, w_out.shape[1])


def solution(mesh):
    placed = (
        P(("grp", "rep", "head"), "seq", None),
        P(None, "head"),
        P("head", None),
        P(("grp", "seq", "rep"), None, None, "head"),
        P(("grp", "seq", "rep"), None, None),
        P(("grp", "seq", "rep"), None, None),
    )
    sizes = dict(mesh.shape)
    n_seq, n_head = sizes["seq"], sizes["head"]

    def body(*arrays):
        local_heads = arrays[1].shape[1] // DH
        if n_head == 2 and sizes["rep"] == 2 and local_heads % n_seq == 0:
            return spread_body(n_seq, n_head, *arrays)
        return plain_body(*arrays)

    return jax.shard_map(
        body,
        mesh=mesh,
        in_specs=placed,
        out_specs=P(("grp", "rep", "head"), "seq", None),
        check_vma=False,
    )
```

```python
import functools

import jax
import jax.numpy as jnp
from jax import lax
from jax.experimental import pallas as pl
from jax.experimental.pallas import tpu as pltpu
from jax.sharding import PartitionSpec as P

DH = 128
BLOCK = 64
KN = 2


def plain_body(tokens, w_query, w_out, neighbour_kv, shard_lists, slot_lists):
    local_seqs, local_span, feature_count = tokens.shape
    local_heads = w_query.shape[1] // DH
    widened = tokens.astype(jnp.float32)
    normed = (
        widened * lax.rsqrt(jnp.mean(widened * widened, axis=2, keepdims=True) + 1e-06)
    ).astype(jnp.bfloat16)
    product = jnp.einsum(
        "std,dh->sth",
        lax.all_gather(normed, "head", axis=0, tiled=True),
        w_query,
        preferred_element_type=jnp.float32,
    )
    queries = (product * DH ** (-0.5)).astype(jnp.bfloat16)
    seq_rep = queries.shape[0]
    own_blocks = seq_rep * local_span // BLOCK
    queries = queries.reshape(own_blocks, BLOCK, local_heads, DH)
    store_count = neighbour_kv.shape[0]
    row_shape = neighbour_kv.shape[1:]
    wanted = shard_lists[0] * store_count + slot_lists[0]
    pieces = lax.all_gather(neighbour_kv, "seq", axis=0, tiled=True)
    fetched = jnp.take(pieces, wanted.reshape(-1), axis=0).reshape((own_blocks, KN) + row_shape)
    key_rows = fetched[:, :, 0].reshape(own_blocks, KN * row_shape[1], local_heads, DH)
    value_rows = fetched[:, :, 1].reshape(own_blocks, KN * row_shape[1], local_heads, DH)
    scores = jnp.einsum("oqhd,okhd->ohqk", queries, key_rows, preferred_element_type=jnp.float32)
    weights = jax.nn.softmax(scores, axis=-1).astype(jnp.bfloat16)
    context = jnp.einsum(
        "ohqk,okhd->oqhd", weights, value_rows, preferred_element_type=jnp.float32
    ).astype(jnp.bfloat16)
    context = context.reshape(seq_rep, local_span, local_heads * DH)
    return lax.psum_scatter(
        jnp.einsum("sth,hd->std", context, w_out, preferred_element_type=jnp.float32).astype(
            jnp.bfloat16
        ),
        "head",
        scatter_dimension=0,
        tiled=True,
    )


MESH = pl.DeviceIdType.MESH
ROW_TILE = 512
CHUNKS = 4
LAG = 2
NORM_TILE = 32


def flow_kernel(
    n_seq, n_head, tokens, w_query, w_out, kv, lists,
    normed, w_out_other,
    context, store, q_in, q_out, c_out, wq_own, wq_other, lists_in, picks,
    kv_send, kv_recv, q_send, q_recv, c_send, c_recv, w_send, w_recv, l_send, l_recv, local, token_sem,
    own_sem, load_sem,
):
    s = lax.axis_index("seq")
    x = lax.axis_index("head")
    r = lax.axis_index("rep")
    rows, features = tokens.shape
    count = kv.shape[0]
    width = q_in.shape[2]
    heads = width // DH
    blocks = rows // BLOCK
    pieces = n_seq * n_head

    def peer(dz, dx):
        return {
            "seq": lax.rem(s + dz + n_seq, n_seq),
            "head": lax.rem(x + dx + n_head, n_head),
        }

    def cols(index):
        return pl.ds(pl.multiple_of(index * width, width), width)

    def remote(src, dst, send, recv, device):
        return pltpu.make_async_remote_copy(
            src_ref=src, dst_ref=dst, send_sem=send, recv_sem=recv, device_id=device, device_id_type=MESH
        )

    barrier = pltpu.get_barrier_semaphore()
    for p in range(1, pieces):
        pl.semaphore_signal(barrier, inc=1, device_id=peer(p // n_head, p % n_head), device_id_type=MESH)
    pl.semaphore_signal(barrier, inc=1, device_id={"rep": 1 - r}, device_id_type=MESH)
    pl.semaphore_wait(barrier, pieces)

    def kv_copy(dz):
        to = lax.rem(s + dz, n_seq)
        return remote(
            kv.at[:, :, :, cols(to)], store.at[pl.ds(s * count, count)],
            kv_send.at[dz], kv_recv.at[dz], peer(dz, 0),
        )

    def list_copy(dz):
        return remote(lists, lists_in.at[dz], l_send.at[dz], l_recv.at[dz], peer(dz, 0))

    chunk_rows = rows // CHUNKS
    chunk_blocks = blocks // CHUNKS

    def chunk_span(c):
        return pl.ds(pl.multiple_of(c * chunk_rows, chunk_rows), chunk_rows)

    def q_copy(p, c):
        span = chunk_span(c)
        return remote(
            q_out.at[p, span], q_in.at[p, span], q_send.at[p, c], q_recv.at[p, c],
            peer(p // n_head, p % n_head),
        )

    def c_copy(p, c):
        dz, dx = p // n_head, p % n_head
        span = chunk_span(c)
        return remote(
            c_out.at[p, span], context.at[dx, span, cols(s)], c_send.at[p, c], c_recv.at[p, c],
            peer(-dz, -dx),
        )

    def own_copy(c):
        span = chunk_span(c)
        return pltpu.make_async_copy(
            c_out.at[0, span], context.at[0, span, cols(s)], own_sem.at[c]
        )

    local_width = w_out.shape[0]
    out_tiles = features // local_width

    def w_load(source, target, which, t):
        return pltpu.make_async_copy(
            source.at[:, pl.ds(t * local_width, local_width)],
            target.at[pl.ds(t * local_width, local_width)],
            load_sem.at[which, t],
        )

    def far_piece(u):
        dz = lax.rem(u // n_head + n_seq // 2 - 1, n_seq - 1) + 1
        return dz * n_head + (n_head - 1 - lax.rem(u, n_head))

    far = (n_seq - 1) * n_head
    far_order = [(t + n_seq // 2 - 1) % (n_seq - 1) + 1 for t in range(n_seq - 1)]

    half = features // 2
    wq_rows = pl.ds(pl.multiple_of(r * half, half), half)
    wq_x = remote(w_query.at[wq_rows], wq_other.at[wq_rows], w_send.at[0], w_recv.at[0], peer(0, 1))
    wq_c = remote(
        wq_other.at[wq_rows], wq_other.at[wq_rows], w_send.at[1], w_recv.at[1], {"rep": 1 - r}
    )
    wo_half = w_out.shape[0] // 2
    wo_rows = pl.ds(pl.multiple_of(r * wo_half, wo_half), wo_half)
    wo_x = remote(w_out.at[wo_rows], w_out_other.at[wo_rows], w_send.at[2], w_recv.at[2], peer(0, 1))
    wo_c = remote(
        w_out_other.at[wo_rows], w_out_other.at[wo_rows], w_send.at[3], w_recv.at[3], {"rep": 1 - r}
    )

    tiles = 4
    tile_rows = rows // tiles
    token_copies = [
        pltpu.make_async_copy(
            tokens.at[pl.ds(t * tile_rows, tile_rows)], normed.at[pl.ds(t * tile_rows, tile_rows)],
            token_sem.at[t],
        )
        for t in range(tiles)
    ]
    wq_local = pltpu.make_async_copy(w_query, wq_own, local.at[0])
    kv_local = pltpu.make_async_copy(
        kv.at[:, :, :, cols(s)], store.at[pl.ds(s * count, count)], local.at[1]
    )
    list_local = pltpu.make_async_copy(lists, lists_in.at[0], local.at[2])

    wq_x.start()
    for copy in token_copies:
        copy.start()
    for dz in range(1, n_seq):
        list_copy(dz).start()
    for dz in far_order:
        kv_copy(dz).start()
    wq_local.start()
    list_local.start()
    kv_local.start()

    def norm(t, carry):
        span = pl.ds(pl.multiple_of(t * NORM_TILE, NORM_TILE), NORM_TILE)
        wide = normed[span, :].astype(jnp.float32)
        scale = lax.rsqrt(jnp.mean(wide * wide, axis=1, keepdims=True) + 1e-06)
        normed[span, :] = (wide * scale).astype(jnp.bfloat16)
        return carry

    per_tile = tile_rows // NORM_TILE
    for t in range(tiles):
        token_copies[t].wait()
        lax.fori_loop(t * per_tile, (t + 1) * per_tile, norm, 0)

    def project(w, to, dst):
        def tile(t, carry):
            span = pl.ds(pl.multiple_of(t * ROW_TILE, ROW_TILE), ROW_TILE)
            product = jnp.dot(normed[span, :], w[:, cols(to)], preferred_element_type=jnp.float32)
            dst[span, :] = (product * DH ** (-0.5)).astype(jnp.bfloat16)
            return carry

        lax.fori_loop(0, rows // ROW_TILE, tile, 0)

    def project_all(w, dx, first):
        def one(dz, carry):
            project(w, lax.rem(s + dz, n_seq), q_out.at[dz * n_head + dx])
            return carry

        lax.fori_loop(first, n_seq, one, 0)

    wq_local.wait()
    project(wq_own, s, q_in.at[0])
    project_all(wq_own, 0, 1)
    for t in range(out_tiles):
        w_load(w_out, wq_own, 0, t).start()
    wq_x.wait_recv()
    wo_x.start()
    wq_c.start()
    wq_c.wait_recv()
    project_all(wq_other, 1, 0)
    for c in range(CHUNKS):
        q_copy(1, c).start()
    for dz in range(1, n_seq):
        kv_copy(dz).wait_send()

    def q_start(t, carry):
        q_copy(far_piece(lax.rem(t, far)), t // far).start()
        return carry

    lax.fori_loop(0, far * CHUNKS, q_start, 0)

    list_local.wait()
    for dz in range(1, n_seq):
        list_copy(dz).wait_recv()
    picks_copy = pltpu.make_async_copy(lists_in, picks, local.at[3])
    picks_copy.start()
    picks_copy.wait()
    kv_local.wait()
    for dz in range(1, n_seq):
        kv_copy(dz).wait_recv()
    wo_x.wait_recv()
    wo_c.start()
    wq_x.wait_send()
    wq_c.wait_send()

    blank = jnp.zeros((BLOCK, DH), jnp.bfloat16)

    def attend(p, c):
        dz, dx = p // n_head, p % n_head
        base = lax.rem(x - dx + n_head, n_head) * blocks

        def step(block, carry):
            block = c * chunk_blocks + block
            at = (base + block) * KN
            chosen = [picks[dz, 0, at + k] for k in range(KN)]
            keys = jnp.concatenate([store[i, 0] for i in chosen], axis=0)
            values = jnp.concatenate([store[i, 1] for i in chosen], axis=0)
            span = pl.ds(pl.multiple_of(block * BLOCK, BLOCK), BLOCK)
            q = q_in[p, span, :]
            spread = jnp.concatenate(
                [
                    jnp.concatenate(
                        [q[:, h * DH:(h + 1) * DH] if h == g else blank for h in range(heads)], axis=1
                    )
                    for g in range(heads)
                ],
                axis=0,
            )
            scores = lax.dot_general(
                spread, keys, (((1,), (1,)), ((), ())), preferred_element_type=jnp.float32
            )
            grown = jnp.exp(scores - jnp.max(scores, axis=-1, keepdims=True))
            weights = (grown / jnp.sum(grown, axis=-1, keepdims=True)).astype(jnp.bfloat16)
            mixed = jnp.dot(weights, values, preferred_element_type=jnp.float32)
            c_out[p, span, :] = jnp.concatenate(
                [mixed[h * BLOCK:(h + 1) * BLOCK, h * DH:(h + 1) * DH] for h in range(heads)], axis=1
            ).astype(jnp.bfloat16)
            return carry

        lax.fori_loop(0, chunk_blocks, step, 0, unroll=4 if chunk_blocks % 4 == 0 else 1)

    def output(c):
        span = chunk_span(c)
        own_copy(c).wait()
        for p in range(1, pieces):
            c_copy(p, c).wait_recv()

        def tile(t, carry):
            depth = pl.ds(pl.multiple_of(t * local_width, local_width), local_width)
            total = jnp.zeros((chunk_rows, local_width), jnp.float32)
            for dx, w in enumerate((wq_own, wq_other)):
                term = jnp.dot(context[dx, span, :], w[depth, :], preferred_element_type=jnp.float32)
                total = total + term.astype(jnp.bfloat16).astype(jnp.float32)
            normed[span, depth] = total.astype(jnp.bfloat16)
            return carry

        lax.fori_loop(0, out_tiles, tile, 0)

    def turn(c, carry):
        @pl.when(c < CHUNKS)
        def _():
            attend(0, c)
            own_copy(c).start()

            def one(t, carry):
                p = jnp.where(t == 0, 1, far_piece(jnp.maximum(t - 1, 0)))
                q_copy(p, c).wait_recv()
                attend(p, c)
                c_copy(p, c).start()
                return carry

            lax.fori_loop(0, pieces - 1, one, 0)

        @pl.when(c == LAG)
        def _():
            wo_c.wait_recv()
            for t in range(out_tiles):
                w_load(w_out_other, wq_other, 1, t).start()
            for t in range(out_tiles):
                w_load(w_out, wq_own, 0, t).wait()
                w_load(w_out_other, wq_other, 1, t).wait()

        @pl.when(c >= LAG)
        def _():
            output(c - LAG)

        return carry

    lax.fori_loop(0, CHUNKS + LAG, turn, 0)

    for dz in range(1, n_seq):
        list_copy(dz).wait_send()
    for copy in (wo_x, wo_c):
        copy.wait_send()

    def drain(t, carry):
        p, c = t // CHUNKS + 1, lax.rem(t, CHUNKS)
        q_copy(p, c).wait_send()
        c_copy(p, c).wait_send()
        return carry

    lax.fori_loop(0, (pieces - 1) * CHUNKS, drain, 0)


def spread_body(n_seq, n_head, tokens, w_query, w_out, neighbour_kv, shard_lists, slot_lists):
    local_seqs, local_span, features = tokens.shape
    rows = local_seqs * local_span
    local_width = w_query.shape[1]
    width = local_width // n_seq
    count, _, length, _ = neighbour_kv.shape
    pieces = n_seq * n_head
    places = (shard_lists[0] * count + slot_lists[0]).reshape(1, -1).astype(jnp.int32)
    lanes = -(-places.shape[1] // 128) * 128
    places = jnp.pad(places, ((0, 7), (0, lanes - places.shape[1])))
    bf16 = jnp.bfloat16
    anywhere = pl.BlockSpec(memory_space=pl.ANY)
    dma = pltpu.SemaphoreType.DMA
    crossed, _ = pl.pallas_call(
        functools.partial(flow_kernel, n_seq, n_head),
        out_shape=[
            pltpu.VMEM((rows, w_out.shape[1]), bf16),
            jax.ShapeDtypeStruct(w_out.shape, bf16),
        ],
        in_specs=[anywhere] * 4 + [pl.BlockSpec(memory_space=pltpu.VMEM)],
        out_specs=[pl.BlockSpec(memory_space=pltpu.VMEM), anywhere],
        scratch_shapes=[
            pltpu.VMEM((n_head, rows, local_width), bf16),
            pltpu.VMEM((n_seq * count, 2, length, width), bf16),
            pltpu.VMEM((pieces, rows, width), bf16),
            pltpu.VMEM((pieces, rows, width), bf16),
            pltpu.VMEM((pieces, rows, width), bf16),
            pltpu.VMEM((features, local_width), bf16),
            pltpu.VMEM((features, local_width), bf16),
            pltpu.VMEM((n_seq, 8, lanes), jnp.int32),
            pltpu.SMEM((n_seq, 8, lanes), jnp.int32),
            dma((n_seq,)), dma((n_seq,)),
            dma((pieces, CHUNKS)), dma((pieces, CHUNKS)),
            dma((pieces, CHUNKS)), dma((pieces, CHUNKS)),
            dma((4,)), dma((4,)),
            dma((n_seq,)), dma((n_seq,)),
            dma((4,)), dma((4,)),
            dma((CHUNKS,)), dma((2, features // local_width)),
        ],
        compiler_params=pltpu.CompilerParams(
            collective_id=0, has_side_effects=True, vmem_limit_bytes=48 * 2**20
        ),
        cost_estimate=pl.CostEstimate(
            flops=2 * rows * features * local_width * n_head, bytes_accessed=2**26, transcendentals=2**22
        ),
        name="flow",
    )(tokens.reshape(rows, features), w_query, w_out, neighbour_kv, places)
    return crossed.reshape(local_seqs, local_span, w_out.shape[1])


def solution(mesh):
    placed = (
        P(("grp", "rep", "head"), "seq", None),
        P(None, "head"),
        P("head", None),
        P(("grp", "seq", "rep"), None, None, "head"),
        P(("grp", "seq", "rep"), None, None),
        P(("grp", "seq", "rep"), None, None),
    )
    sizes = dict(mesh.shape)
    n_seq, n_head = sizes["seq"], sizes["head"]

    def body(*arrays):
        local_heads = arrays[1].shape[1] // DH
        if n_head == 2 and sizes["rep"] == 2 and local_heads % n_seq == 0:
            return spread_body(n_seq, n_head, *arrays)
        return plain_body(*arrays)

    return jax.shard_map(
        body,
        mesh=mesh,
        in_specs=placed,
        out_specs=P(("grp", "rep", "head"), "seq", None),
        check_vma=False,
    )
```
